256 devices in a mesh: role: 2 (over core), req: 16 (over x, y), tp: 8 (over z).
Axes of the slice: x: 4, y: 4, z: 8, core: 2. Of those that a mesh axis runs over, the one named last changes fastest.
Arguments:
- decode_hidden: bfloat16 [2, 128, 8192], P('role', None, 'req'), may hold values from -400 to 400
- span_hidden: bfloat16 [2, 1024, 8192], P('role', 'req'), may hold values from -400 to 400
- norm_gain: bfloat16 [8192], replicated, may hold values from 0.25 to 1.75
- w_query: bfloat16 [8192, 8192], P('req', 'tp'), may hold values from -0.0625 to 0.0625
- w_keyval: bfloat16 [8192, 2048], P(None, 'tp'), may hold values from -0.0625 to 0.0625
- w_out: bfloat16 [8192, 8192], P('tp', 'req'), may hold values from -0.0625 to 0.0625
- cache: bfloat16 [2, 128, 1024, 2048], P('role', 'req', None, 'tp'), may hold values from -400 to 400
- lengths: int32 [2, 128], P('role', 'req'), may hold values from 128 to 1024, as said below
- route: int32 [2, 1024, 3], P('role', 'req'), may hold values from 0 to 127, as said below
Outputs:
- decoded: bfloat16 [2, 128, 8192], P('role', None, 'req')
The draws below stay inside these ranges and needn't reach their ends.
Inputs may be any that keep to these rules, and one draw needn't show every extreme that they name: `route`: each row is (owner, request, slot): owner < 32 names pool owner // 16, request < 8 counts among that owner's requests, slot < 128. No two rows share owner, request and slot. Of the 64 rows of one device, at most 4 go to one owner, and one owner receives exactly 4 from every device. `lengths`: some request has exactly 1024.
All inputs are finite; a program needn't handle non-finite values.
Results may differ from the reference program's by a relative error of at most 0.034.
Values may be sent and summed in bfloat16 or wider, within the bound.
A program may use at most 128 MiB of HBM per device.

```python
import math
import jax
import jax.numpy as jnp
from jax import lax

D = 8192
QH = 64
KVH = 8
HD = 128
REQ_DEV = 8
CTX = 1024
SPAN_DEV = 64
STEPS = 2
POOLS = 2
REQS = 128
SPAN = 1024
CAP = 4


def spread_rows(key, shape, lowest, highest):
    first, second, third = jax.random.split(key, 3)
    width = shape[-1]
    base = jax.random.normal(first, shape, jnp.float32)
    row_scale = jnp.exp(jax.random.uniform(second, shape[:-1] + (1,), jnp.float32, math.log(lowest), math.log(highest)))
    block_of = jnp.arange(width) * 32 // width
    gains = jnp.exp(jax.random.uniform(third, shape[:-1] + (32,), jnp.float32, -1.5, 1.5))
    spread = jnp.take(gains, block_of, axis=-1)
    return jnp.clip(base * row_scale * spread, -400.0, 400.0)


def draw_decode_hidden(key, part):
    key = jax.random.fold_in(key, 1)
    return spread_rows(key, (POOLS, REQS, D), 0.01, 0.2).astype(jnp.bfloat16)


def draw_span_hidden(key, part):
    key = jax.random.fold_in(key, 2)
    return spread_rows(key, (POOLS, SPAN, D), 0.5, 5.0).astype(jnp.bfloat16)


def draw_cache(key, part):
    key = jax.random.fold_in(key, 3)
    first = jax.random.fold_in(key, 0)
    width = KVH * 2 * HD
    return jnp.clip(jax.random.normal(first, (POOLS, REQS, CTX, width), jnp.float32), -6.0, 6.0).astype(jnp.bfloat16)


def draw_lengths(key, part):
    key = jax.random.fold_in(key, 4)
    first, second = jax.random.split(key)
    extent = CTX - 2 * SPAN_DEV
    picked = jax.random.randint(first, (POOLS * REQS,), 0, 1025)
    skewed = picked * picked // 1024 * picked // 1024
    drawn = 2 * SPAN_DEV + extent * skewed // 1024
    chosen = jax.random.randint(second, (), 0, POOLS * REQS)
    drawn = jnp.where(jnp.arange(POOLS * REQS) == chosen, CTX, drawn)
    return drawn.reshape(POOLS, REQS).astype(jnp.int32)


def draw_route(key, part):
    key = jax.random.fold_in(key, 5)
    sources = POOLS * (SPAN // SPAN_DEV)
    owners = sources
    limit = CAP
    key_hot, key_rest, key_req, key_slot = jax.random.split(key, 4)
    hot = jax.random.randint(key_hot, (), 0, owners)
    place = jnp.arange(SPAN_DEV)
    extra = jnp.maximum(place - limit, 0)

    def one_block(block_key):
        key_a, key_b = jax.random.split(block_key)
        others = (hot + 1 + jax.random.permutation(key_a, owners - 1)) % owners
        owner = jnp.where(place < limit, hot, others[extra % (owners - 1)])
        rank = jnp.where(place < limit, place, extra // (owners - 1))
        order = jax.random.permutation(key_b, SPAN_DEV)
        return (owner[order], rank[order])
    owner, rank = jax.vmap(one_block)(jax.random.split(key_rest, sources))
    code = jnp.arange(sources)[:, None] * limit + rank
    tables = jax.vmap(lambda item: jax.random.permutation(item, sources * limit))(jax.random.split(key_slot, owners))
    slot = tables[owner, code]
    request = jax.random.randint(key_req, (sources, SPAN_DEV), 0, REQ_DEV)
    result = jnp.stack([owner, request, slot], axis=-1).reshape(POOLS, SPAN, 3)
    return result.astype(jnp.int32)


def levels(stream_key, shape, cuts, least, top_value):
    factor_of = 1.0
    for axis_at, blocks in cuts:
        draws = jax.random.uniform(jax.random.fold_in(jax.random.fold_in(stream_key, 6), axis_at), (blocks,), jnp.float32, least / len(cuts), top_value / len(cuts))
        factor_of = factor_of * jnp.repeat(jnp.exp(draws), shape[axis_at] // blocks).reshape((-1,) + (1,) * (len(shape) - 1 - axis_at))
    return factor_of


def gaussian(own_key, dims, deviation, bound, cuts=(), kind=jnp.bfloat16):
    level = levels(own_key, dims, cuts, -0.22, 0.18) if cuts else 1.0
    values = jax.random.normal(own_key, dims, jnp.float32) * deviation * level
    return jnp.minimum(jnp.maximum(values, -bound), bound).astype(kind)


def setup_inputs(seed: int = 0) -> dict:
    key_list = jax.random.split(jax.random.key(seed), 10)
    decode_hidden = draw_decode_hidden(jax.random.fold_in(key_list[9], 71), 0)
    span_hidden = draw_span_hidden(jax.random.fold_in(key_list[9], 71), 0)
    norm_gain = jnp.clip(1.0 + 0.15 * jax.random.normal(key_list[2], (D,), jnp.float32), 0.25, 1.75).astype(jnp.bfloat16)
    w_query = gaussian(key_list[3], (D, QH * HD), D ** -0.5, 0.0625, ((0, 16), (1, 8)))
    w_keyval = gaussian(key_list[4], (D, KVH * 2 * HD), D ** -0.5, 0.0625, ((1, 8),))
    w_out = gaussian(key_list[5], (QH * HD, D), (QH * HD) ** -0.5, 0.0625, ((0, 8), (1, 16)))
    cache = draw_cache(jax.random.fold_in(key_list[9], 71), 0)
    lengths = draw_lengths(jax.random.fold_in(key_list[9], 71), 0)
    route = draw_route(jax.random.fold_in(key_list[9], 71), 0)
    return {"decode_hidden": decode_hidden, "span_hidden": span_hidden, "norm_gain": norm_gain, "w_query": w_query, "w_keyval": w_keyval, "w_out": w_out, "cache": cache, "lengths": lengths, "route": route}


EPS = 1e-05
BASE = 500000.0
FLOOR = -1e+30

def rotate(vec, pos):
    half = vec.shape[-1] // 2
    freq = BASE ** (-jnp.arange(half, dtype=jnp.float32) / half)
    angle = pos[..., None].astype(jnp.float32) * freq
    cosine = jnp.cos(angle)
    sine = jnp.sin(angle)
    first = vec[..., :half]
    second = vec[..., half:]
    return jnp.concatenate([first * cosine - second * sine, second * cosine + first * sine], axis=-1)

def scaled_rows(rows, gain):
    wide = rows.astype(jnp.float32)
    scale = lax.rsqrt(lax.optimization_barrier(jnp.mean(wide * wide, axis=-1)) + EPS)
    mixed = (wide * gain.astype(jnp.float32)).astype(jnp.bfloat16)
    return (mixed, scale)

def attend_one(query, rows, length, fresh_keys, fresh_values):
    blocks = rows.reshape(CTX, KVH, 2, HD).astype(jnp.float32)
    keys = blocks[:, :, 0]
    values = blocks[:, :, 1]
    inverse = HD ** (-0.5)
    qwide = query.astype(jnp.float32)
    old = jnp.einsum('gjd,cgd->gjc', qwide, keys) * inverse
    new = jnp.einsum('gjd,ngd->gjn', qwide, fresh_keys.astype(jnp.float32)) * inverse
    live = (jnp.arange(CTX) < length)[None, None, :]
    top = jnp.maximum(lax.optimization_barrier(jnp.max(jnp.where(live, old, FLOOR), axis=-1)), lax.optimization_barrier(jnp.max(new, axis=-1)))
    old_exp = jnp.where(live, jnp.exp(old - top[..., None]), 0.0)
    new_exp = jnp.exp(new - top[..., None])
    total = lax.optimization_barrier(jnp.sum(old_exp, axis=-1)) + lax.optimization_barrier(jnp.sum(new_exp, axis=-1))
    weight_old = (old_exp / total[..., None]).astype(jnp.bfloat16).astype(jnp.float32)
    weight_new = (new_exp / total[..., None]).astype(jnp.bfloat16).astype(jnp.float32)
    out = jnp.einsum('gjc,cgd->gjd', weight_old, values)
    out = out + jnp.einsum('gjn,ngd->gjd', weight_new, fresh_values.astype(jnp.float32))
    return out.astype(jnp.bfloat16).reshape(-1)

def reference(decode_hidden, span_hidden, norm_gain, w_query, w_keyval, w_out, cache, lengths, route):
    handed_rows = []
    flat_index = []
    slot_index = []
    for pool in range(POOLS):
        mixed, scale = scaled_rows(span_hidden[pool], norm_gain)
        keyval = (jnp.dot(mixed, w_keyval, preferred_element_type=jnp.float32) * scale[:, None]).reshape(SPAN, KVH, 2, HD)
        slot = route[pool, :, 2]
        keys = rotate(keyval[:, :, 0], slot[:, None])
        handed_rows.append(jnp.stack([keys, keyval[:, :, 1]], axis=2).reshape(SPAN, -1).astype(jnp.bfloat16))
        flat_index.append((route[pool, :, 0] * REQ_DEV + route[pool, :, 1]).astype(jnp.int32))
        slot_index.append(slot.astype(jnp.int32))
    store = cache.reshape(POOLS * REQS, CTX, KVH * 2 * HD)
    store = store.at[jnp.concatenate(flat_index), jnp.concatenate(slot_index)].set(jnp.concatenate(handed_rows))
    store = store.reshape(POOLS, REQS, CTX, KVH * 2 * HD)
    group = QH // KVH
    outputs = []
    for pool in range(POOLS):
        hidden = decode_hidden[pool]
        fresh_keys = []
        fresh_values = []
        for step in range(STEPS):
            mixed, scale = scaled_rows(hidden, norm_gain)
            query = jnp.dot(mixed, w_query, preferred_element_type=jnp.float32) * scale[:, None]
            keyval = (jnp.dot(mixed, w_keyval, preferred_element_type=jnp.float32) * scale[:, None]).reshape(REQS, KVH, 2, HD)
            position = (lengths[pool] + step)[:, None]
            query = rotate(query.reshape(REQS, QH, HD), position).astype(jnp.bfloat16).reshape(REQS, KVH, group, HD)
            fresh_keys.append(rotate(keyval[:, :, 0], position).astype(jnp.bfloat16))
            fresh_values.append(keyval[:, :, 1].astype(jnp.bfloat16))
            new_keys = jnp.stack(fresh_keys, axis=1)
            new_values = jnp.stack(fresh_values, axis=1)
            heads = lax.map(lambda item: attend_one(*item), (query, store[pool], lengths[pool], new_keys, new_values))
            partial_value = jnp.dot(heads, w_out, preferred_element_type=jnp.float32)
            hidden = (hidden.astype(jnp.float32) + partial_value).astype(jnp.bfloat16)
        outputs.append(hidden)
    return jnp.stack(outputs)
```

```python
import functools
import numpy as np
import jax
import jax.numpy as jnp
from jax import lax
from jax.experimental import pallas as pl
from jax.experimental.pallas import tpu as pltpu
from jax.sharding import PartitionSpec as P

HD = 128
STEPS = 2
EPS = 1e-05
BASE = 500000.0
FLOOR = -1e30
SLOTS = 128
CAP = 4
MESH = pl.DeviceIdType.MESH
F32 = jnp.float32
BF16 = jnp.bfloat16


def iota(shape, axis):
    return lax.broadcasted_iota(jnp.int32, shape, axis)


def dot(a, b):
    return jnp.dot(a, b, preferred_element_type=F32)


def dot_t(a, b):
    return lax.dot_general(a, b, (((1,), (1,)), ((), ())), preferred_element_type=F32)


def to_row(column):
    n = column.shape[0]
    wide = jnp.broadcast_to(column, (n, n))
    return jnp.sum(jnp.where(iota((n, n), 0) == iota((n, n), 1), wide, 0.0), axis=0, keepdims=True)


def to_column(row):
    n = row.shape[1]
    wide = jnp.broadcast_to(row, (n, n))
    return jnp.sum(jnp.where(iota((n, n), 0) == iota((n, n), 1), wide, 0.0), axis=1, keepdims=True)


def angles(pos, freq):
    angle = pos * freq
    sign = jnp.where(iota(angle.shape, 1) < HD // 2, -1.0, 1.0)
    return jnp.cos(angle), jnp.sin(angle) * sign


def turn(vec, cosine, sine):
    return vec * cosine + pltpu.roll(vec, HD // 2, 1) * sine


def kernel(
    dims,
    hid_hbm, span_hbm, gain_hbm, wq_hbm, wkv_hbm, wo_hbm, cache_hbm, len_hbm, route_hbm, freq_hbm,
    out_ref,
    hid, span, gain, wq, wkvs, wkv, wo, cache, lens, route, freq,
    outbox, inbox, proj_out, proj_in, sq, heads_all, part_out, part_in, hid_all, qs, os_,
    load_sem, box_sem, proj_sem, sq_sem, heads_sem, part_sem, hid_sem,
):
    n_role, n_req, n_tp = dims
    role, req, tp = lax.axis_index("role"), lax.axis_index("req"), lax.axis_index("tp")
    owners = n_role * n_req
    me = role * n_req + req
    width = hid.shape[1]
    reqs = hid.shape[0]
    local = reqs // n_req
    ctx = cache.shape[1]
    heads = wq.shape[1] // HD
    rows_tp = reqs // n_tp

    def pool_peer(k):
        other = lax.rem(me + k, owners)
        return other, {"role": other // n_req, "req": lax.rem(other, n_req)}

    def req_peer(k):
        other = lax.rem(req + k, n_req)
        return other, {"req": other}

    def tp_peer(k):
        other = lax.rem(tp + k, n_tp)
        return other, {"tp": other}

    barrier = pltpu.get_barrier_semaphore()
    for k in range(1, owners):
        pl.semaphore_signal(barrier, inc=1, device_id=pool_peer(k)[1], device_id_type=MESH)
    for k in range(1, n_tp):
        pl.semaphore_signal(barrier, inc=1, device_id=tp_peer(k)[1], device_id_type=MESH)

    first = pl.multiple_of(req * width, width)
    loads = {}
    for index, (name, src, dst) in enumerate([
        ("hid", hid_hbm.at[0], hid),
        ("gain", gain_hbm, gain),
        ("wkvs", wkv_hbm.at[pl.ds(first, width)], wkvs),
        ("wq", wq_hbm, wq),
        ("route", route_hbm.at[0], route),
        ("freq", freq_hbm, freq),
        ("lens", len_hbm, lens),
        ("span", span_hbm.at[0], span),
        ("wkv", wkv_hbm, wkv),
        ("cache", cache_hbm.at[0], cache),
        ("wo", wo_hbm, wo),
    ]):
        loads[name] = pltpu.make_async_copy(src, dst, load_sem.at[index])
        loads[name].start()

    def exchange(peers, count, src, dst, send, recv):
        for k in peers:
            other, device = count(k)
            pltpu.make_async_remote_copy(
                src(other), dst, send, recv, device_id=device, device_id_type=MESH
            ).start()

    def wait_bytes(ref, send, recv, device):
        both = pltpu.make_async_remote_copy(ref, ref, send, recv, device_id=device, device_id_type=MESH)
        return both

    def project(rows, step, gain_row):
        wide = rows.astype(F32)
        squares = jnp.sum(wide * wide, axis=1, keepdims=True)
        sq[step, pl.ds(req, 1)] = to_row(squares).reshape(1, 1, reqs)
        mixed = (wide * gain_row).astype(BF16)
        both = jnp.concatenate([dot(mixed, wq[...]), dot(mixed, wkvs[...])], axis=1)
        both = both.reshape(n_req, local, -1)
        half = both.shape[2] // 2
        proj_out[step] = jnp.concatenate([both[:, :, :half], both[:, :, half:]], axis=1).astype(BF16)

    def send_projection(step):
        exchange(range(1, n_req), req_peer, lambda other: sq.at[step, req],
                 sq.at[step, req], sq_sem.at[step, 0], sq_sem.at[step, 1])
        exchange(range(1, n_req), req_peer, lambda other: proj_out.at[step, other],
                 proj_in.at[step, req], proj_sem.at[step, 0], proj_sem.at[step, 1])

    req_one, tp_one, pool_one = req_peer(1)[1], tp_peer(1)[1], pool_peer(1)[1]

    for name in ("hid", "gain", "wkvs", "wq"):
        loads[name].wait()
    gains = gain[...].astype(F32)
    gain_row = jnp.sum(jnp.where(iota(gains.shape, 0) == req, gains, 0.0), axis=0, keepdims=True)
    project(hid[...], 0, gain_row)
    pl.semaphore_wait(barrier, owners + n_tp - 2)
    send_projection(0)

    for name in ("route", "freq", "lens", "span", "wkv"):
        loads[name].wait()
    count = span.shape[0]
    freq_row = freq[0:1, :]
    acc = jnp.zeros((count, 2 * HD), F32)
    squares = jnp.zeros((count, 1), F32)
    for j in range(n_req):
        wide = span[:, j * width:(j + 1) * width].astype(F32)
        squares += jnp.sum(wide * wide, axis=1, keepdims=True)
        acc += dot((wide * gains[j:j + 1, :]).astype(BF16), wkv[j * width:(j + 1) * width, :])
    keyval = acc * lax.rsqrt(squares / (n_req * width) + EPS)
    plan = route[...]
    owner = plan[:, 0:1].astype(F32)
    slot = plan[:, 2:3].astype(F32)
    cosine, sine = angles(slot, freq_row)
    key = turn(keyval[:, :HD], cosine, sine).astype(BF16)
    value = keyval[:, HD:].astype(BF16)
    owner_row = to_row(owner)
    square = (count, count)
    earlier = (iota(square, 0) < iota(square, 1)) & (
        jnp.broadcast_to(owner, square) == jnp.broadcast_to(owner_row, square))
    rank_row = jnp.sum(jnp.where(earlier, 1.0, 0.0), axis=0, keepdims=True)
    place = (owner_row * (4 * CAP) + rank_row).astype(jnp.int32)
    lines = iota((owners * 4 * CAP, count), 0)
    ask = jnp.broadcast_to(plan[:, 1:2].astype(F32) + 1.0, (count, HD)).astype(BF16)
    spot = jnp.broadcast_to(slot, (count, HD)).astype(BF16)
    box = jnp.zeros((owners * 4 * CAP, HD), F32)
    for part, content in enumerate((key, value, ask, spot)):
        pick = jnp.where(lines == place + part * CAP, 1.0, 0.0).astype(BF16)
        box += dot(pick, content)
    outbox[...] = box.astype(BF16)
    chunk = 4 * CAP
    mine = pl.ds(pl.multiple_of(me * chunk, chunk), chunk)
    inbox[mine] = outbox[mine]
    exchange(range(1, owners), pool_peer,
             lambda other: outbox.at[pl.ds(pl.multiple_of(other * chunk, chunk), chunk)],
             inbox.at[mine], box_sem.at[0], box_sem.at[1])

    len_row = lens[...].astype(F32)
    len_col = to_column(len_row)
    tables = [angles(len_col + float(step), freq_row) for step in range(STEPS)]
    pick = (local * heads, local)
    len_rows = jnp.sum(
        jnp.where(iota(pick, 0) // heads == iota(pick, 1),
                  jnp.broadcast_to(len_row, pick), 0.0), axis=1, keepdims=True)

    loads["cache"].wait()
    box_wait = wait_bytes(inbox.at[pl.ds(0, (owners - 1) * chunk)], box_sem.at[0], box_sem.at[1], pool_one)
    box_wait.wait_recv()
    arrived = inbox[...]
    total = owners * CAP
    sel = (4 * total, owners * chunk)
    line = iota(sel, 0)
    part = line // total
    item = lax.rem(line, total)
    want = (item // CAP) * chunk + part * CAP + lax.rem(item, CAP)
    sorted_ = dot(jnp.where(iota(sel, 1) == want, 1.0, 0.0).astype(BF16), arrived)
    key_in = sorted_[0:total].astype(BF16)
    value_in = sorted_[total:2 * total].astype(BF16)
    target = (sorted_[2 * total:3 * total] - 1.0) * float(SLOTS) + sorted_[3 * total:]
    target = jnp.where(sorted_[2 * total:3 * total] > 0.5, target, -1.0)
    target_row = to_row(target[:, 0:1]).astype(jnp.int32)
    ones = jnp.ones((total, HD), BF16)
    for b in range(local):
        hot = jnp.where(iota((SLOTS, total), 0) + b * SLOTS == target_row, 1.0, 0.0).astype(BF16)
        hit = dot(hot, ones) > 0.5
        for lo, rows in ((0, key_in), (HD, value_in)):
            old = cache[b, 0:SLOTS, lo:lo + HD]
            cache[b, 0:SLOTS, lo:lo + HD] = jnp.where(hit, dot(hot, rows), old.astype(F32)).astype(BF16)

    hidden = hid[...]
    fresh = []
    inverse = HD ** (-0.5)
    for step in range(STEPS):
        if step > 0:
            project(hidden, step, gain_row)
            send_projection(step)
        sq_wait = wait_bytes(sq.at[step, pl.ds(0, n_req - 1)], sq_sem.at[step, 0], sq_sem.at[step, 1], req_one)
        proj_wait = wait_bytes(
            proj_in.at[step, pl.ds(0, n_req - 1)], proj_sem.at[step, 0], proj_sem.at[step, 1], req_one)
        proj_in[step, pl.ds(req, 1)] = proj_out[step, pl.ds(req, 1)]
        sq_wait.wait_recv()
        all_squares = jnp.sum(sq[step].reshape(n_req, reqs), axis=0, keepdims=True)
        grid = (local, reqs)
        own = jnp.sum(
            jnp.where(iota(grid, 1) == iota(grid, 0) + req * local,
                      jnp.broadcast_to(all_squares, grid), 0.0), axis=1, keepdims=True)
        scale = lax.rsqrt(own / (n_req * width) + EPS)
        proj_wait.wait_recv()
        summed = proj_in[step, 0].astype(F32)
        for k in range(1, n_req):
            summed += proj_in[step, k].astype(F32)
        half = summed.shape[1]
        flat = jnp.concatenate([summed[:local], summed[local:]], axis=1) * scale
        cosine, sine = tables[step]
        for h in range(heads):
            qs[pl.ds(h, local, stride=heads), :] = turn(flat[:, h * HD:(h + 1) * HD], cosine, sine)
        base = heads * HD
        fresh_key = turn(flat[:, base:base + HD], cosine, sine).astype(BF16).astype(F32)
        fresh_value = flat[:, base + HD:].astype(BF16).astype(F32)
        fresh.append((fresh_key, fresh_value))
        for b in range(local):
            query = qs[b * heads:(b + 1) * heads, :].astype(BF16)
            wide = query.astype(F32)
            news = [
                jnp.sum(wide * k[b:b + 1, :], axis=1, keepdims=True) * inverse for k, _ in fresh
            ]
            old = dot_t(query, cache[b, :, 0:HD]) * inverse
            live = iota((heads, ctx), 1).astype(F32) < len_rows[b * heads:(b + 1) * heads]
            old = jnp.where(live, old, FLOOR)
            top = jnp.max(old, axis=1, keepdims=True)
            for new in news:
                top = jnp.maximum(top, new)
            old_exp = jnp.where(live, jnp.exp(old - top), 0.0)
            new_exp = [jnp.exp(new - top) for new in news]
            norm = jnp.sum(old_exp, axis=1, keepdims=True)
            for item in new_exp:
                norm += item
            mixture = dot(old_exp.astype(BF16), cache[b, :, HD:])
            for item, (_, v) in zip(new_exp, fresh):
                mixture += item.astype(BF16).astype(F32) * v[b:b + 1, :]
            os_[b * heads:(b + 1) * heads, :] = mixture / norm
        pieces = [os_[pl.ds(h, local, stride=heads), :] for h in range(heads)]
        mid = heads // 2
        block = jnp.concatenate(
            [jnp.concatenate(pieces[:mid], axis=1), jnp.concatenate(pieces[mid:], axis=1)], axis=0)
        heads_all[step, pl.ds(req, 1)] = block.astype(BF16).reshape(1, 2 * local, mid * HD)
        exchange(range(1, n_req), req_peer, lambda other: heads_all.at[step, req],
                 heads_all.at[step, req], heads_sem.at[step, 0], heads_sem.at[step, 1])
        if step == 0:
            loads["wo"].wait()
        heads_wait = wait_bytes(
            heads_all.at[step, pl.ds(0, n_req - 1)], heads_sem.at[step, 0], heads_sem.at[step, 1], req_one)
        heads_wait.wait_recv()
        left = heads_all[step].reshape(n_req * 2 * local, mid * HD)
        upper = dot(left, wo[:mid * HD, :]).reshape(n_req, 2 * local, width)
        lower = dot(left, wo[mid * HD:, :]).reshape(n_req, 2 * local, width)
        partial = (upper[:, :local] + lower[:, local:]).reshape(n_tp, rows_tp, width)
        part_out[step] = partial.astype(BF16)
        exchange(range(1, n_tp), tp_peer, lambda other: part_out.at[step, other],
                 part_in.at[step, tp], part_sem.at[step, 0], part_sem.at[step, 1])
        part_in[step, pl.ds(tp, 1)] = part_out[step, pl.ds(tp, 1)]
        part_wait = wait_bytes(
            part_in.at[step, pl.ds(0, n_tp - 1)], part_sem.at[step, 0], part_sem.at[step, 1], tp_one)
        part_wait.wait_recv()
        rows = pl.ds(pl.multiple_of(tp * rows_tp, rows_tp), rows_tp)
        before = hid[rows, :] if step == 0 else hid_all[rows, :]
        summed = part_in[step, 0].astype(F32)
        for k in range(1, n_tp):
            summed += part_in[step, k].astype(F32)
        after = (before.astype(F32) + summed).astype(BF16)
        if step < STEPS - 1:
            dst = hid_all
            hid_all[rows, :] = after
        else:
            dst = out_ref.at[0]
            out_ref[0, rows, :] = after
        exchange(range(1, n_tp), tp_peer, lambda other: dst.at[rows], dst.at[rows],
                 hid_sem.at[step, 0], hid_sem.at[step, 1])
        hid_wait = wait_bytes(
            dst.at[pl.ds(0, (n_tp - 1) * rows_tp)], hid_sem.at[step, 0], hid_sem.at[step, 1], tp_one)
        hid_wait.wait_recv()
        if step < STEPS - 1:
            hidden = hid_all[...]
        for item in (sq_wait, proj_wait, heads_wait, part_wait, hid_wait):
            item.wait_send()
    box_wait.wait_send()


def on_device(dims, decode_hidden, span_hidden, norm_gain, w_query, w_keyval, w_out, cache, lengths, route):
    n_role, n_req, n_tp = dims
    owners = n_role * n_req
    _, reqs, width = decode_hidden.shape
    _, count, _ = span_hidden.shape
    local = reqs // n_req
    cols = w_query.shape[1] + w_keyval.shape[1]
    heads = w_query.shape[1] // HD
    half = HD // 2
    table = np.power(np.float32(BASE), -np.arange(half, dtype=np.float32) / np.float32(half))
    freq = jnp.asarray(np.tile(table.astype(np.float32), (8, 2)))
    any_spec = pl.BlockSpec(memory_space=pl.ANY)
    vmem = pltpu.VMEM
    sems = pltpu.SemaphoreType.DMA
    return pl.pallas_call(
        functools.partial(kernel, dims),
        out_shape=jax.ShapeDtypeStruct(decode_hidden.shape, BF16),
        in_specs=[any_spec] * 10,
        out_specs=pl.BlockSpec(memory_space=pltpu.VMEM),
        scratch_shapes=[
            vmem((reqs, width), BF16),
            vmem(span_hidden.shape[1:], BF16),
            vmem((n_req, width), BF16),
            vmem(w_query.shape, BF16),
            vmem((width, w_keyval.shape[1]), BF16),
            vmem(w_keyval.shape, BF16),
            vmem(w_out.shape, BF16),
            vmem(cache.shape[1:], BF16),
            vmem(lengths.shape, jnp.int32),
            vmem(route.shape[1:], jnp.int32),
            vmem(freq.shape, F32),
            vmem((owners * 4 * CAP, HD), BF16),
            vmem((owners * 4 * CAP, HD), BF16),
            vmem((STEPS, n_req, 2 * local, cols // 2), BF16),
            vmem((STEPS, n_req, 2 * local, cols // 2), BF16),
            vmem((STEPS, n_req, 1, reqs), F32),
            vmem((STEPS, n_req, 2 * local, heads * HD // 2), BF16),
            vmem((STEPS, n_tp, reqs // n_tp, width), BF16),
            vmem((STEPS, n_tp, reqs // n_tp, width), BF16),
            vmem((reqs, width), BF16),
            vmem((local * heads, HD), F32),
            vmem((local * heads, HD), F32),
            sems((11,)),
            sems((2,)),
            sems((STEPS, 2)),
            sems((STEPS, 2)),
            sems((STEPS, 2)),
            sems((STEPS, 2)),
            sems((STEPS, 2)),
        ],
        compiler_params=pltpu.CompilerParams(
            collective_id=0, has_side_effects=True, vmem_limit_bytes=56 * 2**20
        ),
        name="decode",
    )(decode_hidden, span_hidden, norm_gain.reshape(n_req, width), w_query, w_keyval, w_out, cache,
      lengths, route, freq)


def solution(mesh):
    dims = tuple(mesh.shape[name] for name in ("role", "req", "tp"))
    placed = (
        P("role", None, "req"),
        P("role", "req", None),
        P(),
        P("req", "tp"),
        P(None, "tp"),
        P("tp", "req"),
        P("role", "req", None, "tp"),
        P("role", "req"),
        P("role", "req", None),
    )
    return jax.shard_map(
        functools.partial(on_device, dims), mesh=mesh, in_specs=placed,
        out_specs=P("role", None, "req"), check_vma=False,
    )
```

```python
import functools
import numpy as np
import jax
import jax.numpy as jnp
from jax import lax
from jax.experimental import pallas as pl
from jax.experimental.pallas import tpu as pltpu
from jax.sharding import PartitionSpec as P

HD = 128
STEPS = 2
EPS = 1e-05
BASE = 500000.0
FLOOR = -1e30
SLOTS = 128
CAP = 4
MESH = pl.DeviceIdType.MESH
F32 = jnp.float32
BF16 = jnp.bfloat16


def iota(shape, axis):
    return lax.broadcasted_iota(jnp.int32, shape, axis)


def dot(a, b):
    return jnp.dot(a, b, preferred_element_type=F32)


def dot_t(a, b):
    return lax.dot_general(a, b, (((1,), (1,)), ((), ())), preferred_element_type=F32)


def to_row(column):
    n = column.shape[0]
    wide = jnp.broadcast_to(column, (n, n))
    return jnp.sum(jnp.where(iota((n, n), 0) == iota((n, n), 1), wide, 0.0), axis=0, keepdims=True)


def to_column(row):
    n = row.shape[1]
    wide = jnp.broadcast_to(row, (n, n))
    return jnp.sum(jnp.where(iota((n, n), 0) == iota((n, n), 1), wide, 0.0), axis=1, keepdims=True)


def angles(pos, freq):
    angle = pos * freq
    sign = jnp.where(iota(angle.shape, 1) < HD // 2, -1.0, 1.0)
    return jnp.cos(angle), jnp.sin(angle) * sign


def turn(vec, cosine, sine):
    return vec * cosine + pltpu.roll(vec, HD // 2, 1) * sine


def kernel(
    dims,
    hid_hbm, span_hbm, gain_hbm, wq_hbm, wkv_hbm, wo_hbm, cache_hbm, len_hbm, route_hbm, freq_hbm,
    out_ref,
    hid, span, gain, wq, wkvs, wkv, wo, cache, lens, route, freq,
    outbox, inbox, proj_out, proj_in, heads_all, part_out, part_in, hid_all, qs, os_,
    load_sem, box_sem, proj_sem, heads_sem, part_sem, hid_sem,
):
    n_role, n_req, n_tp = dims
    role, req, tp = lax.axis_index("role"), lax.axis_index("req"), lax.axis_index("tp")
    owners = n_role * n_req
    me = role * n_req + req
    width = hid.shape[1]
    reqs = hid.shape[0]
    local = reqs // n_req
    ctx = cache.shape[1]
    heads = wq.shape[1] // HD
    rows_tp = reqs // n_tp

    side = int(n_req ** 0.5)

    def far(k, n):
        return min(k, n - k)

    steps = [(a, b) for a in range(side) for b in range(side)]
    steps.sort(key=lambda s: -far(s[0], side) - far(s[1], side))
    req_steps = steps[:-1]
    pool_steps = [(flip, s) for s in steps for flip in (False, True)]
    pool_steps.remove((False, (0, 0)))
    tp_steps = sorted(range(1, n_tp), key=lambda k: -far(k, n_tp))

    def req_peer(step, flip=False):
        other = lax.rem(req // side + step[0], side) * side + lax.rem(lax.rem(req, side) + step[1], side)
        return other, {"role": 1 - role if flip else role, "req": other}

    def pool_peer(step):
        other, device = req_peer(step[1], step[0])
        return device["role"] * n_req + other, device

    def tp_peer(k):
        other = lax.rem(tp + k, n_tp)
        return other, {"tp": other}

    first = pl.multiple_of(req * width, width)
    loads = {}
    arrays = [
        ("hid", hid_hbm.at[0], hid),
        ("gain", gain_hbm, gain),
        ("wkvs", wkv_hbm.at[pl.ds(first, width)], wkvs),
        ("wq", wq_hbm, wq),
        ("route", route_hbm, route),
        ("freq", freq_hbm, freq),
        ("lens", len_hbm, lens),
        ("span", span_hbm.at[0], span),
        ("wkv", wkv_hbm, wkv),
        ("cache", cache_hbm.at[0], cache),
        ("wo", wo_hbm, wo),
    ]

    def load(some):
        for index in some:
            name, src, dst = arrays[index]
            loads[name] = pltpu.make_async_copy(src, dst, load_sem.at[index])
            loads[name].start()

    load(range(4))
    barrier = pltpu.get_barrier_semaphore()
    greeted = [pool_peer(k)[1] for k in pool_steps]
    greeted += [tp_peer(k)[1] for k in tp_steps]
    for device in greeted:
        pl.semaphore_signal(barrier, inc=1, device_id=device, device_id_type=MESH)
    load(range(4, len(arrays)))

    def exchange(peers, peer, src, dst, sems):
        for k in peers:
            other, device = peer(k)
            pltpu.make_async_remote_copy(
                src(other), dst, sems.at[0], sems.at[1], device_id=device, device_id_type=MESH
            ).start()

    def arrivals(ref, sems):
        return pltpu.make_async_remote_copy(
            ref, ref, sems.at[0], sems.at[1], device_id=req_peer(steps[0])[1], device_id_type=MESH
        )

    def project(rows, step, gain_row):
        wide = rows.astype(F32)
        squares = jnp.sum(wide * wide, axis=1, keepdims=True)
        squares = jnp.broadcast_to(squares, (reqs, HD)).reshape(n_req, local, HD)
        main = squares.astype(BF16).astype(F32)
        mixed = (wide * gain_row).astype(BF16)
        both = jnp.concatenate([dot(mixed, wq[...]), dot(mixed, wkvs[...])], axis=1)
        both = both.reshape(n_req, local, -1)
        half = both.shape[2] // 2
        upper = jnp.concatenate([both[:, :, :half], main], axis=2)
        lower = jnp.concatenate([both[:, :, half:], squares - main], axis=2)
        proj_out[step] = jnp.concatenate([upper, lower], axis=1).astype(BF16)

    def send_projection(step):
        exchange(req_steps, req_peer, lambda other: proj_out.at[step, other],
                 proj_in.at[step, req], proj_sem.at[step])

    for name in ("hid", "gain", "wkvs", "wq"):
        loads[name].wait()
    gains = jnp.concatenate(
        [gain[j * width:(j + 1) * width].astype(F32).reshape(1, width) for j in range(n_req)], axis=0)
    gain_row = jnp.sum(jnp.where(iota(gains.shape, 0) == req, gains, 0.0), axis=0, keepdims=True)
    project(hid[...], 0, gain_row)
    pl.semaphore_wait(barrier, len(greeted))
    send_projection(0)

    for name in ("route", "freq", "lens", "span", "wkv"):
        loads[name].wait()
    count = span.shape[0]
    freq_row = freq[0:1, :]
    acc = jnp.zeros((count, 2 * HD), F32)
    squares = jnp.zeros((count, 1), F32)
    for j in range(n_req):
        wide = span[:, j * width:(j + 1) * width].astype(F32)
        squares += jnp.sum(wide * wide, axis=1, keepdims=True)
        acc += dot((wide * gains[j:j + 1, :]).astype(BF16), wkv[j * width:(j + 1) * width, :])
    keyval = acc * lax.rsqrt(squares / (n_req * width) + EPS)
    owner_row, ask, slot = (route[j].astype(F32) for j in range(3))
    owner, ask, slot = to_column(owner_row), to_column(ask), to_column(slot)
    cosine, sine = angles(slot, freq_row)
    key = turn(keyval[:, :HD], cosine, sine).astype(BF16)
    value = keyval[:, HD:].astype(BF16)
    square = (count, count)
    earlier = (iota(square, 0) < iota(square, 1)) & (
        jnp.broadcast_to(owner, square) == jnp.broadcast_to(owner_row, square))
    rank_row = jnp.sum(jnp.where(earlier, 1.0, 0.0), axis=0, keepdims=True)
    place = (owner_row * (4 * CAP) + rank_row).astype(jnp.int32)
    lines = iota((owners * 4 * CAP, count), 0)
    ask = jnp.broadcast_to(ask + 1.0, (count, HD)).astype(BF16)
    spot = jnp.broadcast_to(slot, (count, HD)).astype(BF16)
    box = jnp.zeros((owners * 4 * CAP, HD), F32)
    for part, content in enumerate((key, value, ask, spot)):
        pick = jnp.where(lines == place + part * CAP, 1.0, 0.0).astype(BF16)
        box += dot(pick, content)
    outbox[...] = box.astype(BF16)
    chunk = 4 * CAP
    mine = pl.ds(pl.multiple_of(me * chunk, chunk), chunk)
    inbox[mine] = outbox[mine]
    exchange(pool_steps, pool_peer,
             lambda other: outbox.at[pl.ds(pl.multiple_of(other * chunk, chunk), chunk)],
             inbox.at[mine], box_sem)

    len_row = lens[...].astype(F32)
    len_col = to_column(len_row)
    tables = [angles(len_col + float(step), freq_row) for step in range(STEPS)]
    pick = (local * heads, local)
    len_rows = jnp.sum(
        jnp.where(iota(pick, 0) // heads == iota(pick, 1),
                  jnp.broadcast_to(len_row, pick), 0.0), axis=1, keepdims=True)

    def place_handed():
        arrived = inbox[...]
        total = owners * CAP
        sel = (4 * total, owners * chunk)
        line = iota(sel, 0)
        part = line // total
        item = lax.rem(line, total)
        want = (item // CAP) * chunk + part * CAP + lax.rem(item, CAP)
        sorted_ = dot(jnp.where(iota(sel, 1) == want, 1.0, 0.0).astype(BF16), arrived)
        key_in = sorted_[0:total].astype(BF16)
        value_in = sorted_[total:2 * total].astype(BF16)
        target = (sorted_[2 * total:3 * total] - 1.0) * float(SLOTS) + sorted_[3 * total:]
        target = jnp.where(sorted_[2 * total:3 * total] > 0.5, target, -1.0)
        target_row = to_row(target[:, 0:1]).astype(jnp.int32)
        ones = jnp.ones((total, HD), BF16)
        for b in range(local):
            hot = jnp.where(iota((SLOTS, total), 0) + b * SLOTS == target_row, 1.0, 0.0).astype(BF16)
            hit = dot(hot, ones) > 0.5
            for lo, rows in ((0, key_in), (HD, value_in)):
                old = cache[b, 0:SLOTS, lo:lo + HD]
                cache[b, 0:SLOTS, lo:lo + HD] = jnp.where(hit, dot(hot, rows), old.astype(F32)).astype(BF16)

    loads["cache"].wait()
    box_wait = arrivals(inbox.at[pl.ds(0, (owners - 1) * chunk)], box_sem)
    sent = [box_wait]
    fresh = []
    inverse = HD ** (-0.5)
    many = local * heads
    hidden = hid
    for step in range(STEPS):
        last = step == STEPS - 1
        if step > 0:
            project(hidden[...], step, gain_row)
            send_projection(step)
        proj_wait = arrivals(proj_in.at[step, pl.ds(0, n_req - 1)], proj_sem.at[step])
        proj_in[step, pl.ds(req, 1)] = proj_out[step, pl.ds(req, 1)]
        proj_wait.wait_recv()
        summed = proj_in[step, 0].astype(F32)
        for k in range(1, n_req):
            summed += proj_in[step, k].astype(F32)
        half = summed.shape[1] - HD
        own = summed[:local, half:half + 1] + summed[local:, half:half + 1]
        scale = lax.rsqrt(own / (n_req * width) + EPS)
        flat = jnp.concatenate([summed[:local, :half], summed[local:, :half]], axis=1) * scale
        cosine, sine = tables[step]
        for h in range(heads):
            qs[pl.ds(h, local, stride=heads), :] = turn(flat[:, h * HD:(h + 1) * HD], cosine, sine)
        base = heads * HD

        def spread(rows):
            rows = rows.astype(BF16).astype(F32)
            return jnp.broadcast_to(rows[:, None, :], (local, heads, HD)).reshape(many, HD)

        fresh.append((spread(turn(flat[:, base:base + HD], cosine, sine)), spread(flat[:, base + HD:])))
        queries = [qs[b * heads:(b + 1) * heads, :].astype(BF16) for b in range(local)]

        def scores(lo, hi):
            return jnp.concatenate(
                [dot_t(queries[b], cache[b, lo:hi, 0:HD]) for b in range(local)], axis=0) * inverse

        late = scores(SLOTS, ctx)
        live = iota(late.shape, 1) + SLOTS < len_rows
        late = jnp.where(live, late, FLOOR)
        if step == 0:
            box_wait.wait_recv()
            place_handed()
        early = scores(0, SLOTS)
        wide = qs[...].astype(BF16).astype(F32)
        news = [jnp.sum(wide * k, axis=1, keepdims=True) * inverse for k, _ in fresh]
        top = jnp.maximum(jnp.max(late, axis=1, keepdims=True), jnp.max(early, axis=1, keepdims=True))
        for new in news:
            top = jnp.maximum(top, new)
        early, late = jnp.exp(early - top), jnp.exp(late - top)
        norm = jnp.sum(early, axis=1, keepdims=True) + jnp.sum(late, axis=1, keepdims=True)
        weights = jnp.concatenate([early, late], axis=1)
        mixture = jnp.concatenate([
            dot(weights[b * heads:(b + 1) * heads].astype(BF16), cache[b, :, HD:]) for b in range(local)
        ], axis=0)
        for new, (_, v) in zip(news, fresh):
            new = jnp.exp(new - top)
            norm += new
            mixture += new.astype(BF16).astype(F32) * v
        os_[...] = mixture / norm
        pieces = [os_[pl.ds(h, local, stride=heads), :] for h in range(heads)]
        mid = heads // 2
        block = jnp.concatenate(
            [jnp.concatenate(pieces[:mid], axis=1), jnp.concatenate(pieces[mid:], axis=1)], axis=0)
        heads_all[step, pl.ds(req, 1)] = block.astype(BF16).reshape(1, 2 * local, mid * HD)
        exchange(req_steps, req_peer, lambda other: heads_all.at[step, req],
                 heads_all.at[step, req], heads_sem.at[step])
        if step == 0:
            loads["wo"].wait()
        heads_wait = arrivals(heads_all.at[step, pl.ds(0, n_req - 1)], heads_sem.at[step])
        heads_wait.wait_recv()
        left = heads_all[step].reshape(n_req * 2 * local, mid * HD)
        upper = dot(left, wo[:mid * HD, :]).reshape(n_req, 2 * local, width)
        lower = dot(left, wo[mid * HD:, :]).reshape(n_req, 2 * local, width)
        partial = (upper[:, :local] + lower[:, local:]).reshape(n_tp, rows_tp, width)
        part_out[step] = partial.astype(BF16)
        exchange(tp_steps, tp_peer, lambda other: part_out.at[step, other],
                 part_in.at[step, tp], part_sem.at[step])
        part_in[step, pl.ds(tp, 1)] = part_out[step, pl.ds(tp, 1)]
        part_wait = arrivals(part_in.at[step, pl.ds(0, n_tp - 1)], part_sem.at[step])
        part_wait.wait_recv()
        rows = pl.ds(pl.multiple_of(tp * rows_tp, rows_tp), rows_tp)
        summed = hidden[rows, :].astype(F32)
        for k in range(n_tp):
            summed += part_in[step, k].astype(F32)
        target = out_ref.at[0] if last else hid_all
        target[rows, :] = summed.astype(BF16)
        exchange(tp_steps, tp_peer, lambda other: target.at[rows], target.at[rows], hid_sem.at[step])
        hid_wait = arrivals(target.at[pl.ds(0, (n_tp - 1) * rows_tp)], hid_sem.at[step])
        hid_wait.wait_recv()
        hidden = hid_all
        sent += [proj_wait, heads_wait, part_wait, hid_wait]
    for item in sent:
        item.wait_send()


def on_device(dims, decode_hidden, span_hidden, norm_gain, w_query, w_keyval, w_out, cache, lengths, route):
    n_role, n_req, n_tp = dims
    owners = n_role * n_req
    _, reqs, width = decode_hidden.shape
    _, count, _ = span_hidden.shape
    local = reqs // n_req
    cols = w_query.shape[1] + w_keyval.shape[1]
    heads = w_query.shape[1] // HD
    half = HD // 2
    table = np.power(np.float32(BASE), -np.arange(half, dtype=np.float32) / np.float32(half))
    freq = jnp.asarray(np.tile(table.astype(np.float32), (8, 2)))
    any_spec = pl.BlockSpec(memory_space=pl.ANY)
    vmem = pltpu.VMEM
    sems = pltpu.SemaphoreType.DMA
    return pl.pallas_call(
        functools.partial(kernel, dims),
        out_shape=pltpu.VMEM(decode_hidden.shape, BF16),
        in_specs=[any_spec] * 10,
        out_specs=pl.BlockSpec(memory_space=pltpu.VMEM),
        scratch_shapes=[
            vmem((reqs, width), BF16),
            vmem(span_hidden.shape[1:], BF16),
            vmem(norm_gain.shape, BF16),
            vmem(w_query.shape, BF16),
            vmem((width, w_keyval.shape[1]), BF16),
            vmem(w_keyval.shape, BF16),
            vmem(w_out.shape, BF16),
            vmem(cache.shape[1:], BF16),
            vmem(lengths.shape, jnp.int32),
            vmem((3, 1, count), jnp.int32),
            vmem(freq.shape, F32),
            vmem((owners * 4 * CAP, HD), BF16),
            vmem((owners * 4 * CAP, HD), BF16),
            vmem((STEPS, n_req, 2 * local, cols // 2 + HD), BF16),
            vmem((STEPS, n_req, 2 * local, cols // 2 + HD), BF16),
            vmem((STEPS, n_req, 2 * local, heads * HD // 2), BF16),
            vmem((STEPS, n_tp, reqs // n_tp, width), BF16),
            vmem((STEPS, n_tp, reqs // n_tp, width), BF16),
            vmem((reqs, width), BF16),
            vmem((local * heads, HD), F32),
            vmem((local * heads, HD), F32),
            sems((11,)),
            sems((2,)),
            sems((STEPS, 2)),
            sems((STEPS, 2)),
            sems((STEPS, 2)),
            sems((STEPS, 2)),
        ],
        compiler_params=pltpu.CompilerParams(
            collective_id=0, has_side_effects=True, vmem_limit_bytes=56 * 2**20
        ),
        name="decode",
    )(decode_hidden, span_hidden, norm_gain, w_query, w_keyval, w_out, cache,
      lengths, jnp.transpose(route, (2, 0, 1)), freq)


def solution(mesh):
    dims = tuple(mesh.shape[name] for name in ("role", "req", "tp"))
    placed = (
        P("role", None, "req"),
        P("role", "req", None),
        P(),
        P("req", "tp"),
        P(None, "tp"),
        P("tp", "req"),
        P("role", "req", None, "tp"),
        P("role", "req"),
        P("role", "req", None),
    )
    return jax.shard_map(
        functools.partial(on_device, dims), mesh=mesh, in_specs=placed,
        out_specs=P("role", None, "req"), check_vma=False,
    )
```

```python
import functools
import numpy as np
import jax
import jax.numpy as jnp
from jax import lax
from jax.experimental import pallas as pl
from jax.experimental.pallas import tpu as pltpu
from jax.sharding import PartitionSpec as P

HD = 128
STEPS = 2
EPS = 1e-05
BASE = 500000.0
FLOOR = -1e30
SLOTS = 128
CAP = 4
MESH = pl.DeviceIdType.MESH
F32 = jnp.float32
BF16 = jnp.bfloat16


def iota(shape, axis):
    return lax.broadcasted_iota(jnp.int32, shape, axis)


def dot(a, b):
    return jnp.dot(a, b, preferred_element_type=F32)


def dot_t(a, b):
    return lax.dot_general(a, b, (((1,), (1,)), ((), ())), preferred_element_type=F32)


def to_row(column):
    n = column.shape[0]
    wide = jnp.broadcast_to(column, (n, n))
    return jnp.sum(jnp.where(iota((n, n), 0) == iota((n, n), 1), wide, 0.0), axis=0, keepdims=True)


def to_column(row):
    n = row.shape[1]
    wide = jnp.broadcast_to(row, (n, n))
    return jnp.sum(jnp.where(iota((n, n), 0) == iota((n, n), 1), wide, 0.0), axis=1, keepdims=True)


def angles(pos, freq):
    angle = pos * freq
    sign = jnp.where(iota(angle.shape, 1) < HD // 2, -1.0, 1.0)
    return jnp.cos(angle), jnp.sin(angle) * sign


def turn(vec, cosine, sine):
    return vec * cosine + pltpu.roll(vec, HD // 2, 1) * sine


def kernel(
    dims,
    hid_hbm, span_hbm, gain_hbm, wq_hbm, wkv_hbm, wo_hbm, cache_hbm, len_hbm, route_hbm, freq_hbm,
    out_ref,
    hid, span, gain, wq, wkvs, wkv, wo, cache, lens, route, freq,
    outbox, inbox, proj_out, proj_in, sq, heads_all, part_out, part_in, hid_all, qs, os_,
    load_sem, box_sem, proj_sem, sq_sem, heads_sem, part_sem, hid_sem,
):
    n_role, n_req, n_tp = dims
    role, req, tp = lax.axis_index("role"), lax.axis_index("req"), lax.axis_index("tp")
    owners = n_role * n_req
    me = role * n_req + req
    width = hid.shape[1]
    reqs = hid.shape[0]
    local = reqs // n_req
    ctx = cache.shape[1]
    heads = wq.shape[1] // HD
    rows_tp = reqs // n_tp

    side = int(n_req ** 0.5)

    def far(k, n):
        return min(k, n - k)

    steps = [(a, b) for a in range(side) for b in range(side)]
    steps.sort(key=lambda s: -far(s[0], side) - far(s[1], side))
    req_steps = steps[:-1] if side != 4 else [(2, 2), (1, 2), (3, 2), (2, 1), (2, 3), (1, 1), (3, 3), (1, 3), (3, 1), (0, 2), (2, 0), (0, 1), (0, 3), (1, 0), (3, 0)]
    pool_steps = [(flip, s) for flip in (False, True) for s in req_steps + [(0, 0)]]
    pool_steps.remove((False, (0, 0)))
    tp_steps = sorted(range(1, n_tp), key=lambda k: -far(k, n_tp))

    def req_peer(step, flip=False):
        other = lax.rem(req // side + step[0], side) * side + lax.rem(lax.rem(req, side) + step[1], side)
        return other, {"role": 1 - role if flip else role, "req": other}

    def pool_peer(step):
        other, device = req_peer(step[1], step[0])
        return device["role"] * n_req + other, device

    def tp_peer(k):
        other = lax.rem(tp + k, n_tp)
        return other, {"tp": other}

    first = pl.multiple_of(req * width, width)
    loads = {}
    arrays = [
        ("hid", hid_hbm.at[0], hid),
        ("gain", gain_hbm, gain),
        ("wkvs", wkv_hbm.at[pl.ds(first, width)], wkvs),
        ("wq", wq_hbm, wq),
        ("route", route_hbm, route),
        ("freq", freq_hbm, freq),
        ("lens", len_hbm, lens),
        ("span", span_hbm.at[0], span),
        ("wkv", wkv_hbm, wkv),
        ("cache", cache_hbm.at[0], cache),
        ("wo", wo_hbm, wo),
    ]

    def load(some):
        for index in some:
            name, src, dst = arrays[index]
            loads[name] = pltpu.make_async_copy(src, dst, load_sem.at[index])
            loads[name].start()

    barrier = pltpu.get_barrier_semaphore()
    greeted = [pool_peer(k)[1] for k in pool_steps]
    greeted += [tp_peer(k)[1] for k in tp_steps]
    for device in greeted:
        pl.semaphore_signal(barrier, inc=1, device_id=device, device_id_type=MESH)
    load(range(len(arrays)))

    def exchange(peers, peer, src, dst, sems):
        for k in peers:
            other, device = peer(k)
            pltpu.make_async_remote_copy(
                src(other), dst, sems.at[0], sems.at[1], device_id=device, device_id_type=MESH
            ).start()

    def arrivals(ref, sems):
        return pltpu.make_async_remote_copy(
            ref, ref, sems.at[0], sems.at[1], device_id=req_peer(steps[0])[1], device_id_type=MESH
        )

    def project(rows, step, gain_row):
        wide = rows.astype(F32)
        mixed = (wide * gain_row).astype(BF16)
        both = jnp.concatenate([dot(mixed, wq[...]), dot(mixed, wkvs[...])], axis=1)
        both = both.reshape(n_req, local, -1)
        half = both.shape[2] // 2
        proj_out[step] = jnp.concatenate([both[:, :, :half], both[:, :, half:]], axis=1).astype(BF16)

    def send_projection(rows, step):
        exchange(req_steps, req_peer, lambda other: proj_out.at[step, other],
                 proj_in.at[step, req], proj_sem.at[step])
        wide = rows.astype(F32)
        sq[step, pl.ds(req, 1)] = to_row(jnp.sum(wide * wide, axis=1, keepdims=True)).reshape(1, 1, reqs)
        exchange(req_steps, req_peer, lambda other: sq.at[step, req], sq.at[step, req], sq_sem.at[step])

    for name in ("hid", "gain", "wkvs", "wq"):
        loads[name].wait()
    gains = jnp.concatenate(
        [gain[j * width:(j + 1) * width].astype(F32).reshape(1, width) for j in range(n_req)], axis=0)
    gain_row = jnp.sum(jnp.where(iota(gains.shape, 0) == req, gains, 0.0), axis=0, keepdims=True)
    project(hid[...], 0, gain_row)
    pl.semaphore_wait(barrier, len(greeted))
    send_projection(hid[...], 0)

    for name in ("route", "freq", "lens", "span", "wkv"):
        loads[name].wait()
    count = span.shape[0]
    freq_row = freq[0:1, :]
    acc = jnp.zeros((count, 2 * HD), F32)
    squares = jnp.zeros((count, 1), F32)
    for j in range(n_req):
        wide = span[:, j * width:(j + 1) * width].astype(F32)
        squares += jnp.sum(wide * wide, axis=1, keepdims=True)
        acc += dot((wide * gains[j:j + 1, :]).astype(BF16), wkv[j * width:(j + 1) * width, :])
    keyval = acc * lax.rsqrt(squares / (n_req * width) + EPS)
    owner_row, ask, slot = (route[j].astype(F32) for j in range(3))
    owner, ask, slot = to_column(owner_row), to_column(ask), to_column(slot)
    cosine, sine = angles(slot, freq_row)
    key = turn(keyval[:, :HD], cosine, sine).astype(BF16)
    value = keyval[:, HD:].astype(BF16)
    square = (count, count)
    earlier = (iota(square, 0) < iota(square, 1)) & (
        jnp.broadcast_to(owner, square) == jnp.broadcast_to(owner_row, square))
    rank_row = jnp.sum(jnp.where(earlier, 1.0, 0.0), axis=0, keepdims=True)
    place = (owner_row * (4 * CAP) + rank_row).astype(jnp.int32)
    lines = iota((owners * 4 * CAP, count), 0)
    ask = jnp.broadcast_to(ask + 1.0, (count, HD)).astype(BF16)
    spot = jnp.broadcast_to(slot, (count, HD)).astype(BF16)
    box = jnp.zeros((owners * 4 * CAP, HD), F32)
    for part, content in enumerate((key, value, ask, spot)):
        pick = jnp.where(lines == place + part * CAP, 1.0, 0.0).astype(BF16)
        box += dot(pick, content)
    outbox[...] = box.astype(BF16)
    chunk = 4 * CAP
    mine = pl.ds(pl.multiple_of(me * chunk, chunk), chunk)
    inbox[mine] = outbox[mine]
    exchange(pool_steps, pool_peer,
             lambda other: outbox.at[pl.ds(pl.multiple_of(other * chunk, chunk), chunk)],
             inbox.at[mine], box_sem)

    len_row = lens[...].astype(F32)
    len_col = to_column(len_row)
    tables = [angles(len_col + float(step), freq_row) for step in range(STEPS)]
    pick = (local * heads, local)
    len_rows = jnp.sum(
        jnp.where(iota(pick, 0) // heads == iota(pick, 1),
                  jnp.broadcast_to(len_row, pick), 0.0), axis=1, keepdims=True)

    def place_handed():
        arrived = inbox[...]
        total = owners * CAP
        sel = (4 * total, owners * chunk)
        line = iota(sel, 0)
        part = line // total
        item = lax.rem(line, total)
        want = (item // CAP) * chunk + part * CAP + lax.rem(item, CAP)
        sorted_ = dot(jnp.where(iota(sel, 1) == want, 1.0, 0.0).astype(BF16), arrived)
        ask, spot = sorted_[2 * total:3 * total], sorted_[3 * total:]
        target = jnp.where(ask > 0.5, (ask - 1.0) * float(SLOTS) + spot, -1.0)
        eye = iota((total, total), 0) == iota((total, total), 1)
        target_row = jnp.sum(jnp.where(eye, target[:, :total], 0.0), axis=0, keepdims=True).astype(jnp.int32)
        handed = jnp.concatenate(
            [sorted_[0:total], sorted_[total:2 * total], jnp.ones((total, HD), F32)], axis=1).astype(BF16)
        hot = jnp.where(iota((local * SLOTS, total), 0) == target_row, 1.0, 0.0).astype(BF16)
        put = dot(hot, handed).reshape(local, SLOTS, 3 * HD)
        hit = put[:, :, 2 * HD:] > 0.5
        old = cache[:, 0:SLOTS, :].astype(F32)
        cache[:, 0:SLOTS, :] = jnp.concatenate(
            [jnp.where(hit, put[:, :, 0:HD], old[:, :, 0:HD]),
             jnp.where(hit, put[:, :, HD:2 * HD], old[:, :, HD:])], axis=2).astype(BF16)

    loads["cache"].wait()
    box_wait = arrivals(inbox.at[pl.ds(0, (owners - 1) * chunk)], box_sem)
    sent = [box_wait]
    fresh = []
    inverse = HD ** (-0.5)
    many = local * heads
    hidden = hid
    for step in range(STEPS):
        last = step == STEPS - 1
        if step > 0:
            project(hidden[...], step, gain_row)
            send_projection(hidden[...], step)
        proj_wait = arrivals(proj_in.at[step, pl.ds(0, n_req - 1)], proj_sem.at[step])
        proj_in[step, pl.ds(req, 1)] = proj_out[step, pl.ds(req, 1)]
        sq_wait = arrivals(sq.at[step, pl.ds(0, n_req - 1)], sq_sem.at[step])
        sq_wait.wait_recv()
        squares = jnp.sum(sq[step].reshape(n_req, reqs), axis=0, keepdims=True)
        grid = (local, reqs)
        own = jnp.sum(
            jnp.where(iota(grid, 1) == iota(grid, 0) + req * local,
                      jnp.broadcast_to(squares, grid), 0.0), axis=1, keepdims=True)
        scale = lax.rsqrt(own / (n_req * width) + EPS)
        proj_wait.wait_recv()
        summed = proj_in[step, 0].astype(F32)
        for k in range(1, n_req):
            summed += proj_in[step, k].astype(F32)
        flat = jnp.concatenate([summed[:local], summed[local:]], axis=1) * scale
        cosine, sine = tables[step]
        for h in range(heads):
            qs[pl.ds(h, local, stride=heads), :] = turn(flat[:, h * HD:(h + 1) * HD], cosine, sine)
        base = heads * HD

        def spread(rows):
            rows = rows.astype(BF16).astype(F32)
            return jnp.broadcast_to(rows[:, None, :], (local, heads, HD)).reshape(many, HD)

        fresh.append((spread(turn(flat[:, base:base + HD], cosine, sine)), spread(flat[:, base + HD:])))
        queries = [qs[b * heads:(b + 1) * heads, :].astype(BF16) for b in range(local)]

        def scores(lo, hi):
            return jnp.concatenate(
                [dot_t(queries[b], cache[b, lo:hi, 0:HD]) for b in range(local)], axis=0) * inverse

        late = scores(SLOTS, ctx)
        live = iota(late.shape, 1) + SLOTS < len_rows
        late = jnp.where(live, late, FLOOR)
        if step == 0:
            box_wait.wait_recv()
            place_handed()
        early = scores(0, SLOTS)
        wide = qs[...].astype(BF16).astype(F32)
        news = [jnp.sum(wide * k, axis=1, keepdims=True) * inverse for k, _ in fresh]
        top = jnp.maximum(jnp.max(late, axis=1, keepdims=True), jnp.max(early, axis=1, keepdims=True))
        for new in news:
            top = jnp.maximum(top, new)
        early, late = jnp.exp(early - top), jnp.exp(late - top)
        norm = jnp.sum(early, axis=1, keepdims=True) + jnp.sum(late, axis=1, keepdims=True)
        weights = jnp.concatenate([early, late], axis=1)
        mixture = jnp.concatenate([
            dot(weights[b * heads:(b + 1) * heads].astype(BF16), cache[b, :, HD:]) for b in range(local)
        ], axis=0)
        for new, (_, v) in zip(news, fresh):
            new = jnp.exp(new - top)
            norm += new
            mixture += new.astype(BF16).astype(F32) * v
        os_[...] = mixture / norm
        pieces = [os_[pl.ds(h, local, stride=heads), :] for h in range(heads)]
        mid = heads // 2
        block = jnp.concatenate(
            [jnp.concatenate(pieces[:mid], axis=1), jnp.concatenate(pieces[mid:], axis=1)], axis=0)
        heads_all[step, pl.ds(req, 1)] = block.astype(BF16).reshape(1, 2 * local, mid * HD)
        exchange(req_steps, req_peer, lambda other: heads_all.at[step, req],
                 heads_all.at[step, req], heads_sem.at[step])
        if step == 0:
            loads["wo"].wait()
        heads_wait = arrivals(heads_all.at[step, pl.ds(0, n_req - 1)], heads_sem.at[step])
        heads_wait.wait_recv()
        left = heads_all[step].reshape(n_req * 2 * local, mid * HD)
        upper = dot(left, wo[:mid * HD, :]).reshape(n_req, 2 * local, width)
        lower = dot(left, wo[mid * HD:, :]).reshape(n_req, 2 * local, width)
        partial = (upper[:, :local] + lower[:, local:]).reshape(n_tp, rows_tp, width)
        part_out[step] = partial.astype(BF16)
        exchange(tp_steps, tp_peer, lambda other: part_out.at[step, other],
                 part_in.at[step, tp], part_sem.at[step])
        part_in[step, pl.ds(tp, 1)] = part_out[step, pl.ds(tp, 1)]
        part_wait = arrivals(part_in.at[step, pl.ds(0, n_tp - 1)], part_sem.at[step])
        part_wait.wait_recv()
        rows = pl.ds(pl.multiple_of(tp * rows_tp, rows_tp), rows_tp)
        summed = hidden[rows, :].astype(F32)
        for k in range(n_tp):
            summed += part_in[step, k].astype(F32)
        target = out_ref.at[0] if last else hid_all
        target[rows, :] = summed.astype(BF16)
        exchange(tp_steps, tp_peer, lambda other: target.at[rows], target.at[rows], hid_sem.at[step])
        hid_wait = arrivals(target.at[pl.ds(0, (n_tp - 1) * rows_tp)], hid_sem.at[step])
        hid_wait.wait_recv()
        hidden = hid_all
        sent += [sq_wait, proj_wait, heads_wait, part_wait, hid_wait]
    for item in sent:
        item.wait_send()


def on_device(dims, decode_hidden, span_hidden, norm_gain, w_query, w_keyval, w_out, cache, lengths, route):
    n_role, n_req, n_tp = dims
    owners = n_role * n_req
    _, reqs, width = decode_hidden.shape
    _, count, _ = span_hidden.shape
    local = reqs // n_req
    cols = w_query.shape[1] + w_keyval.shape[1]
    heads = w_query.shape[1] // HD
    half = HD // 2
    table = np.power(np.float32(BASE), -np.arange(half, dtype=np.float32) / np.float32(half))
    freq = jnp.asarray(np.tile(table.astype(np.float32), (8, 2)))
    any_spec = pl.BlockSpec(memory_space=pl.ANY)
    vmem = pltpu.VMEM
    sems = pltpu.SemaphoreType.DMA
    return pl.pallas_call(
        functools.partial(kernel, dims),
        out_shape=pltpu.VMEM(decode_hidden.shape, BF16),
        in_specs=[any_spec] * 10,
        out_specs=pl.BlockSpec(memory_space=pltpu.VMEM),
        scratch_shapes=[
            vmem((reqs, width), BF16),
            vmem(span_hidden.shape[1:], BF16),
            vmem(norm_gain.shape, BF16),
            vmem(w_query.shape, BF16),
            vmem((width, w_keyval.shape[1]), BF16),
            vmem(w_keyval.shape, BF16),
            vmem(w_out.shape, BF16),
            vmem(cache.shape[1:], BF16),
            vmem(lengths.shape, jnp.int32),
            vmem((3, 1, count), jnp.int32),
            vmem(freq.shape, F32),
            vmem((owners * 4 * CAP, HD), BF16),
            vmem((owners * 4 * CAP, HD), BF16),
            vmem((STEPS, n_req, 2 * local, cols // 2), BF16),
            vmem((STEPS, n_req, 2 * local, cols // 2), BF16),
            vmem((STEPS, n_req, 1, reqs), F32),
            vmem((STEPS, n_req, 2 * local, heads * HD // 2), BF16),
            vmem((STEPS, n_tp, reqs // n_tp, width), BF16),
            vmem((STEPS, n_tp, reqs // n_tp, width), BF16),
            vmem((reqs, width), BF16),
            vmem((local * heads, HD), F32),
            vmem((local * heads, HD), F32),
            sems((11,)),
            sems((2,)),
            sems((STEPS, 2)),
            sems((STEPS, 2)),
            sems((STEPS, 2)),
            sems((STEPS, 2)),
            sems((STEPS, 2)),
        ],
        compiler_params=pltpu.CompilerParams(
            collective_id=0, has_side_effects=True, vmem_limit_bytes=56 * 2**20
        ),
        name="decode",
    )(decode_hidden, span_hidden, norm_gain, w_query, w_keyval, w_out, cache,
      lengths, jnp.transpose(route, (2, 0, 1)), freq)


def solution(mesh):
    dims = tuple(mesh.shape[name] for name in ("role", "req", "tp"))
    placed = (
        P("role", None, "req"),
        P("role", "req", None),
        P(),
        P("req", "tp"),
        P(None, "tp"),
        P("tp", "req"),
        P("role", "req", None, "tp"),
        P("role", "req"),
        P("role", "req", None),
    )
    return jax.shard_map(
        functools.partial(on_device, dims), mesh=mesh, in_specs=placed,
        out_specs=P("role", None, "req"), check_vma=False,
    )
```

```python
import functools
import numpy as np
import jax
import jax.numpy as jnp
from jax import lax
from jax.experimental import pallas as pl
from jax.experimental.pallas import tpu as pltpu
from jax.sharding import PartitionSpec as P

HD = 128
STEPS = 2
EPS = 1e-05
BASE = 500000.0
FLOOR = -1e30
SLOTS = 128
CAP = 4
MESH = pl.DeviceIdType.MESH
F32 = jnp.float32
BF16 = jnp.bfloat16


def iota(shape, axis):
    return lax.broadcasted_iota(jnp.int32, shape, axis)


def dot(a, b):
    return jnp.dot(a, b, preferred_element_type=F32)


def dot_t(a, b):
    return lax.dot_general(a, b, (((1,), (1,)), ((), ())), preferred_element_type=F32)


def to_row(column):
    n = column.shape[0]
    wide = jnp.broadcast_to(column, (n, n))
    return jnp.sum(jnp.where(iota((n, n), 0) == iota((n, n), 1), wide, 0.0), axis=0, keepdims=True)


def to_column(row):
    n = row.shape[1]
    wide = jnp.broadcast_to(row, (n, n))
    return jnp.sum(jnp.where(iota((n, n), 0) == iota((n, n), 1), wide, 0.0), axis=1, keepdims=True)


def angles(pos, freq):
    angle = pos * freq
    sign = jnp.where(iota(angle.shape, 1) < HD // 2, -1.0, 1.0)
    return jnp.cos(angle), jnp.sin(angle) * sign


def turn(vec, cosine, sine):
    return vec * cosine + pltpu.roll(vec, HD // 2, 1) * sine


def kernel(
    dims,
    hid_hbm, span_hbm, gain_hbm, wq_hbm, wkv_hbm, wo_hbm, cache_hbm, len_hbm, route_hbm, freq_hbm,
    out_ref,
    hid, span, gain, wq, wkvs, wkv, wo, cache, lens, route, freq,
    outbox, inbox, proj_out, proj_in, sq, heads_all, part_out, part_in, hid_all, qs, os_,
    load_sem, box_sem, proj_sem, sq_sem, heads_sem, part_sem, hid_sem,
):
    n_role, n_req, n_tp = dims
    role, req, tp = lax.axis_index("role"), lax.axis_index("req"), lax.axis_index("tp")
    owners = n_role * n_req
    me = role * n_req + req
    width = hid.shape[1]
    reqs = hid.shape[0]
    local = reqs // n_req
    ctx = cache.shape[1]
    heads = wq.shape[1] // HD
    rows_tp = reqs // n_tp

    side = int(n_req ** 0.5)

    def far(k, n):
        return min(k, n - k)

    steps = [(a, b) for a in range(side) for b in range(side)]
    steps.sort(key=lambda s: -far(s[0], side) - far(s[1], side))
    req_steps = steps[:-1] if side != 4 else [(2, 2), (1, 2), (3, 2), (2, 1), (2, 3), (1, 1), (3, 3), (1, 3), (3, 1), (0, 2), (2, 0), (0, 1), (0, 3), (1, 0), (3, 0)]
    pool_steps = [(flip, s) for flip in (False, True) for s in req_steps + [(0, 0)]]
    pool_steps.remove((False, (0, 0)))
    tp_steps = sorted(range(1, n_tp), key=lambda k: -far(k, n_tp))
    if n_tp == 8:
        tp_steps = [4, 3, 5, 6, 2, 1, 7]

    def req_peer(step, flip=False):
        other = lax.rem(req // side + step[0], side) * side + lax.rem(lax.rem(req, side) + step[1], side)
        return other, {"role": 1 - role if flip else role, "req": other}

    def pool_peer(step):
        other, device = req_peer(step[1], step[0])
        return device["role"] * n_req + other, device

    def tp_peer(k):
        other = lax.rem(tp + k, n_tp)
        return other, {"tp": other}

    first = pl.multiple_of(req * width, width)
    loads = {}
    arrays = [
        ("gain", gain_hbm, gain),
        ("hid", hid_hbm.at[0], hid),
        ("wkvs", wkv_hbm.at[pl.ds(first, width)], wkvs),
        ("wq", wq_hbm, wq),
        ("route", route_hbm, route),
        ("freq", freq_hbm, freq),
        ("lens", len_hbm, lens),
        ("span", span_hbm.at[0], span),
        ("wkv", wkv_hbm, wkv),
        ("cache", cache_hbm.at[0], cache),
        ("wo", wo_hbm, wo),
    ]

    def load(some):
        for index in some:
            name, src, dst = arrays[index]
            loads[name] = pltpu.make_async_copy(src, dst, load_sem.at[index])
            loads[name].start()

    barrier = pltpu.get_barrier_semaphore()
    greeted = [pool_peer(k)[1] for k in pool_steps]
    greeted += [tp_peer(k)[1] for k in tp_steps]
    for device in greeted:
        pl.semaphore_signal(barrier, inc=1, device_id=device, device_id_type=MESH)
    load(range(len(arrays)))

    def exchange(peers, peer, src, dst, sems):
        for k in peers:
            other, device = peer(k)
            pltpu.make_async_remote_copy(
                src(other), dst, sems.at[0], sems.at[1], device_id=device, device_id_type=MESH
            ).start()

    def arrivals(ref, sems):
        return pltpu.make_async_remote_copy(
            ref, ref, sems.at[0], sems.at[1], device_id=req_peer(steps[0])[1], device_id_type=MESH
        )

    def project(rows, step, gain_row):
        wide = rows.astype(F32)
        mixed = (wide * gain_row).astype(BF16)
        if step == 0:
            loads["wkvs"].wait()
            loads["wq"].wait()
        both = jnp.concatenate([dot(mixed, wq[...]), dot(mixed, wkvs[...])], axis=1)
        both = both.reshape(n_req, local, -1)
        half = both.shape[2] // 2
        proj_out[step] = jnp.concatenate([both[:, :, :half], both[:, :, half:]], axis=1).astype(BF16)

    def send_projection(rows, step):
        exchange(req_steps, req_peer, lambda other: proj_out.at[step, other],
                 proj_in.at[step, req], proj_sem.at[step])
        wide = rows.astype(F32)
        sq[step, pl.ds(req, 1)] = to_row(jnp.sum(wide * wide, axis=1, keepdims=True)).reshape(1, 1, reqs)
        exchange(req_steps, req_peer, lambda other: sq.at[step, req], sq.at[step, req], sq_sem.at[step])

    loads["gain"].wait()
    gains = jnp.concatenate(
        [gain[j * width:(j + 1) * width].astype(F32).reshape(1, width) for j in range(n_req)], axis=0)
    gain_row = jnp.sum(jnp.where(iota(gains.shape, 0) == req, gains, 0.0), axis=0, keepdims=True)
    loads["hid"].wait()
    project(hid[...], 0, gain_row)
    pl.semaphore_wait(barrier, len(greeted))
    send_projection(hid[...], 0)

    for name in ("route", "freq", "lens", "span", "wkv"):
        loads[name].wait()
    count = span.shape[0]
    freq_row = freq[0:1, :]
    acc = jnp.zeros((count, 2 * HD), F32)
    squares = jnp.zeros((count, 1), F32)
    for j in range(n_req):
        wide = span[:, j * width:(j + 1) * width].astype(F32)
        squares += jnp.sum(wide * wide, axis=1, keepdims=True)
        acc += dot((wide * gains[j:j + 1, :]).astype(BF16), wkv[j * width:(j + 1) * width, :])
    keyval = acc * lax.rsqrt(squares / (n_req * width) + EPS)
    owner_row, ask, slot = (route[j].astype(F32) for j in range(3))
    owner, ask, slot = to_column(owner_row), to_column(ask), to_column(slot)
    cosine, sine = angles(slot, freq_row)
    key = turn(keyval[:, :HD], cosine, sine).astype(BF16)
    value = keyval[:, HD:].astype(BF16)
    square = (count, count)
    earlier = (iota(square, 0) < iota(square, 1)) & (
        jnp.broadcast_to(owner, square) == jnp.broadcast_to(owner_row, square))
    rank_row = jnp.sum(jnp.where(earlier, 1.0, 0.0), axis=0, keepdims=True)
    place = (owner_row * (4 * CAP) + rank_row).astype(jnp.int32)
    lines = iota((owners * 4 * CAP, count), 0)
    ask = jnp.broadcast_to(ask + 1.0, (count, HD)).astype(BF16)
    spot = jnp.broadcast_to(slot, (count, HD)).astype(BF16)
    box = jnp.zeros((owners * 4 * CAP, HD), F32)
    for part, content in enumerate((key, value, ask, spot)):
        pick = jnp.where(lines == place + part * CAP, 1.0, 0.0).astype(BF16)
        box += dot(pick, content)
    outbox[...] = box.astype(BF16)
    chunk = 4 * CAP
    mine = pl.ds(pl.multiple_of(me * chunk, chunk), chunk)
    inbox[mine] = outbox[mine]
    exchange(pool_steps, pool_peer,
             lambda other: outbox.at[pl.ds(pl.multiple_of(other * chunk, chunk), chunk)],
             inbox.at[mine], box_sem)

    len_row = lens[...].astype(F32)
    len_col = to_column(len_row)
    tables = [angles(len_col + float(step), freq_row) for step in range(STEPS)]
    pick = (local * heads, local)
    len_rows = jnp.sum(
        jnp.where(iota(pick, 0) // heads == iota(pick, 1),
                  jnp.broadcast_to(len_row, pick), 0.0), axis=1, keepdims=True)

    def place_handed():
        arrived = inbox[...]
        total = owners * CAP
        sel = (4 * total, owners * chunk)
        line = iota(sel, 0)
        part = line // total
        item = lax.rem(line, total)
        want = (item // CAP) * chunk + part * CAP + lax.rem(item, CAP)
        sorted_ = dot(jnp.where(iota(sel, 1) == want, 1.0, 0.0).astype(BF16), arrived)
        ask, spot = sorted_[2 * total:3 * total], sorted_[3 * total:]
        target = jnp.where(ask > 0.5, (ask - 1.0) * float(SLOTS) + spot, -1.0)
        eye = iota((total, total), 0) == iota((total, total), 1)
        target_row = jnp.sum(jnp.where(eye, target[:, :total], 0.0), axis=0, keepdims=True).astype(jnp.int32)
        handed = jnp.concatenate(
            [sorted_[0:total], sorted_[total:2 * total], jnp.ones((total, HD), F32)], axis=1).astype(BF16)
        hot = jnp.where(iota((local * SLOTS, total), 0) == target_row, 1.0, 0.0).astype(BF16)
        put = dot(hot, handed).reshape(local, SLOTS, 3 * HD)
        hit = put[:, :, 2 * HD:] > 0.5
        old = cache[:, 0:SLOTS, :].astype(F32)
        cache[:, 0:SLOTS, :] = jnp.concatenate(
            [jnp.where(hit, put[:, :, 0:HD], old[:, :, 0:HD]),
             jnp.where(hit, put[:, :, HD:2 * HD], old[:, :, HD:])], axis=2).astype(BF16)

    loads["cache"].wait()
    box_wait = arrivals(inbox.at[pl.ds(0, (owners - 1) * chunk)], box_sem)
    sent = [box_wait]
    fresh = []
    inverse = HD ** (-0.5)
    many = local * heads
    hidden = hid
    for step in range(STEPS):
        last = step == STEPS - 1
        if step > 0:
            project(hidden[...], step, gain_row)
            send_projection(hidden[...], step)
        proj_wait = arrivals(proj_in.at[step, pl.ds(0, n_req - 1)], proj_sem.at[step])
        proj_in[step, pl.ds(req, 1)] = proj_out[step, pl.ds(req, 1)]
        sq_wait = arrivals(sq.at[step, pl.ds(0, n_req - 1)], sq_sem.at[step])
        sq_wait.wait_recv()
        squares = jnp.sum(sq[step].reshape(n_req, reqs), axis=0, keepdims=True)
        grid = (local, reqs)
        own = jnp.sum(
            jnp.where(iota(grid, 1) == iota(grid, 0) + req * local,
                      jnp.broadcast_to(squares, grid), 0.0), axis=1, keepdims=True)
        scale = lax.rsqrt(own / (n_req * width) + EPS)
        proj_wait.wait_recv()
        summed = proj_in[step, 0].astype(F32)
        for k in range(1, n_req):
            summed += proj_in[step, k].astype(F32)
        flat = jnp.concatenate([summed[:local], summed[local:]], axis=1) * scale
        cosine, sine = tables[step]
        for h in range(heads):
            qs[pl.ds(h, local, stride=heads), :] = turn(flat[:, h * HD:(h + 1) * HD], cosine, sine)
        base = heads * HD

        def spread(rows):
            rows = rows.astype(BF16).astype(F32)
            return jnp.broadcast_to(rows[:, None, :], (local, heads, HD)).reshape(many, HD)

        fresh.append((spread(turn(flat[:, base:base + HD], cosine, sine)), spread(flat[:, base + HD:])))
        queries = [qs[b * heads:(b + 1) * heads, :].astype(BF16) for b in range(local)]

        def scores(lo, hi):
            return jnp.concatenate(
                [dot_t(queries[b], cache[b, lo:hi, 0:HD]) for b in range(local)], axis=0) * inverse

        def mix(weights, lo, hi):
            return jnp.concatenate([
                dot(weights[b * heads:(b + 1) * heads].astype(BF16), cache[b, lo:hi, HD:])
                for b in range(local)
            ], axis=0)

        if step == 0:
            late = scores(SLOTS, ctx)
            live = iota(late.shape, 1) + SLOTS < len_rows
            late = jnp.where(live, late, FLOOR)
            wide = qs[...].astype(BF16).astype(F32)
            news = [jnp.sum(wide * k, axis=1, keepdims=True) * inverse for k, _ in fresh]
            first_top = jnp.max(late, axis=1, keepdims=True)
            for new in news:
                first_top = jnp.maximum(first_top, new)
            late = jnp.exp(late - first_top)
            norm = jnp.sum(late, axis=1, keepdims=True)
            mixture = mix(late, SLOTS, ctx)
            for new, (_, v) in zip(news, fresh):
                new = jnp.exp(new - first_top)
                norm += new
                mixture += new.astype(BF16).astype(F32) * v
            box_wait.wait_recv()
            place_handed()
            early = scores(0, SLOTS)
            top = jnp.maximum(first_top, jnp.max(early, axis=1, keepdims=True))
            early = jnp.exp(early - top)
            shrink = jnp.exp(first_top - top)
            norm = norm * shrink + jnp.sum(early, axis=1, keepdims=True)
            mixture = mixture * shrink + mix(early, 0, SLOTS)
        else:
            full = scores(0, ctx)
            full = jnp.where(iota(full.shape, 1) < len_rows, full, FLOOR)
            wide = qs[...].astype(BF16).astype(F32)
            news = [jnp.sum(wide * k, axis=1, keepdims=True) * inverse for k, _ in fresh]
            top = jnp.max(full, axis=1, keepdims=True)
            for new in news:
                top = jnp.maximum(top, new)
            full = jnp.exp(full - top)
            norm = jnp.sum(full, axis=1, keepdims=True)
            mixture = mix(full, 0, ctx)
            for new, (_, v) in zip(news, fresh):
                new = jnp.exp(new - top)
                norm += new
                mixture += new.astype(BF16).astype(F32) * v
        os_[...] = mixture / norm
        pieces = [os_[pl.ds(h, local, stride=heads), :] for h in range(heads)]
        mid = heads // 2
        block = jnp.concatenate(
            [jnp.concatenate(pieces[:mid], axis=1), jnp.concatenate(pieces[mid:], axis=1)], axis=0)
        heads_all[step, pl.ds(req, 1)] = block.astype(BF16).reshape(1, 2 * local, mid * HD)
        exchange(req_steps, req_peer, lambda other: heads_all.at[step, req],
                 heads_all.at[step, req], heads_sem.at[step])
        if step == 0:
            loads["wo"].wait()
        heads_wait = arrivals(heads_all.at[step, pl.ds(0, n_req - 1)], heads_sem.at[step])
        heads_wait.wait_recv()
        left = heads_all[step].reshape(n_req * 2 * local, mid * HD)
        upper = dot(left, wo[:mid * HD, :]).reshape(n_req, 2 * local, width)
        lower = dot(left, wo[mid * HD:, :]).reshape(n_req, 2 * local, width)
        partial = (upper[:, :local] + lower[:, local:]).reshape(n_tp, rows_tp, width)
        part_out[step] = partial.astype(BF16)
        exchange(tp_steps, tp_peer, lambda other: part_out.at[step, other],
                 part_in.at[step, tp], part_sem.at[step])
        part_in[step, pl.ds(tp, 1)] = part_out[step, pl.ds(tp, 1)]
        part_wait = arrivals(part_in.at[step, pl.ds(0, n_tp - 1)], part_sem.at[step])
        part_wait.wait_recv()
        rows = pl.ds(pl.multiple_of(tp * rows_tp, rows_tp), rows_tp)
        summed = hidden[rows, :].astype(F32)
        for k in range(n_tp):
            summed += part_in[step, k].astype(F32)
        target = out_ref.at[0] if last else hid_all
        target[rows, :] = summed.astype(BF16)
        exchange(tp_steps, tp_peer, lambda other: target.at[rows], target.at[rows], hid_sem.at[step])
        hid_wait = arrivals(target.at[pl.ds(0, (n_tp - 1) * rows_tp)], hid_sem.at[step])
        hid_wait.wait_recv()
        hidden = hid_all
        sent += [sq_wait, proj_wait, heads_wait, part_wait, hid_wait]
    for item in sent:
        item.wait_send()


def on_device(dims, decode_hidden, span_hidden, norm_gain, w_query, w_keyval, w_out, cache, lengths, route):
    n_role, n_req, n_tp = dims
    owners = n_role * n_req
    _, reqs, width = decode_hidden.shape
    _, count, _ = span_hidden.shape
    local = reqs // n_req
    cols = w_query.shape[1] + w_keyval.shape[1]
    heads = w_query.shape[1] // HD
    half = HD // 2
    table = np.power(np.float32(BASE), -np.arange(half, dtype=np.float32) / np.float32(half))
    freq = jnp.asarray(np.tile(table.astype(np.float32), (8, 2)))
    any_spec = pl.BlockSpec(memory_space=pl.ANY)
    vmem = pltpu.VMEM
    sems = pltpu.SemaphoreType.DMA
    return pl.pallas_call(
        functools.partial(kernel, dims),
        out_shape=pltpu.VMEM(decode_hidden.shape, BF16),
        in_specs=[any_spec] * 10,
        out_specs=pl.BlockSpec(memory_space=pltpu.VMEM),
        scratch_shapes=[
            vmem((reqs, width), BF16),
            vmem(span_hidden.shape[1:], BF16),
            vmem(norm_gain.shape, BF16),
            vmem(w_query.shape, BF16),
            vmem((width, w_keyval.shape[1]), BF16),
            vmem(w_keyval.shape, BF16),
            vmem(w_out.shape, BF16),
            vmem(cache.shape[1:], BF16),
            vmem(lengths.shape, jnp.int32),
            vmem((3, 1, count), jnp.int32),
            vmem(freq.shape, F32),
            vmem((owners * 4 * CAP, HD), BF16),
            vmem((owners * 4 * CAP, HD), BF16),
            vmem((STEPS, n_req, 2 * local, cols // 2), BF16),
            vmem((STEPS, n_req, 2 * local, cols // 2), BF16),
            vmem((STEPS, n_req, 1, reqs), F32),
            vmem((STEPS, n_req, 2 * local, heads * HD // 2), BF16),
            vmem((STEPS, n_tp, reqs // n_tp, width), BF16),
            vmem((STEPS, n_tp, reqs // n_tp, width), BF16),
            vmem((reqs, width), BF16),
            vmem((local * heads, HD), F32),
            vmem((local * heads, HD), F32),
            sems((11,)),
            sems((2,)),
            sems((STEPS, 2)),
            sems((STEPS, 2)),
            sems((STEPS, 2)),
            sems((STEPS, 2)),
            sems((STEPS, 2)),
        ],
        compiler_params=pltpu.CompilerParams(
            collective_id=0, has_side_effects=True, vmem_limit_bytes=56 * 2**20
        ),
        name="decode",
    )(decode_hidden, span_hidden, norm_gain, w_query, w_keyval, w_out, cache,
      lengths, jnp.transpose(route, (2, 0, 1)), freq)


def solution(mesh):
    dims = tuple(mesh.shape[name] for name in ("role", "req", "tp"))
    placed = (
        P("role", None, "req"),
        P("role", "req", None),
        P(),
        P("req", "tp"),
        P(None, "tp"),
        P("tp", "req"),
        P("role", "req", None, "tp"),
        P("role", "req"),
        P("role", "req", None),
    )
    return jax.shard_map(
        functools.partial(on_device, dims), mesh=mesh, in_specs=placed,
        out_specs=P("role", None, "req"), check_vma=False,
    )
```
